32 devices in a mesh: row: 16 (over z, y, core), col: 2 (over x).
Axes of the slice: x: 2, y: 2, z: 4, core: 2. Of those that a mesh axis runs over, the one named last changes fastest.
Arguments:
- weight: float32 [25600, 5120], P('row', 'col'), may hold values from -6 to 6
- grad: float32 [25600, 5120], P('row', 'col'), may hold values from -6 to 6
- momentum: float32 [25600, 5120], P('row', 'col'), may hold values from -90 to 90
- right_factor: bfloat16 [5120, 256], P('col'), may hold values from -0.078125 to 0.078125
Outputs:
- new_weight: float32 [25600, 5120], P('row', 'col')
- new_momentum: float32 [25600, 5120], P('row', 'col')
- new_right: bfloat16 [5120, 256], P(('col', 'row'))
The draws below stay inside these ranges and needn't reach their ends.
All inputs are finite; a program needn't handle non-finite values.
Results may differ from the reference program's by a relative error of at most 0.0023.
Values sent between devices are 32-bit elements; how exact they have to be, the bound alone decides.
No kernel may reach another device: no remote copies, remote signals or barrier semaphores. Data moves between devices by JAX's collectives and lax.ppermute only.
A program may use at most 128 MiB of HBM per device.

```python
import jax
import jax.numpy as jnp
from jax import lax

M = 25600
N = 5120
R = 256


def draw_momentum(key, part):
    first = jax.random.fold_in(key, 11)
    second = jax.random.fold_in(key, 12)
    third = jax.random.fold_in(key, 13)
    row_scale = 3.0 ** (jnp.arange(M, dtype=jnp.float32) / M) * jnp.exp(jax.random.uniform(first, (M,), jnp.float32, 0.0, jnp.log(4.0)))
    col_scale = 3.0 ** (jnp.arange(N, dtype=jnp.float32) / N) * jnp.exp(jax.random.uniform(second, (N,), jnp.float32, 0.0, jnp.log(10.0)))
    values = jax.random.normal(third, (M, N), jnp.float32)
    values = jnp.clip(values, -5.0, 5.0)
    return (values * row_scale[:, None] * col_scale[None, :] / 20.0).astype(jnp.float32)


def shard_levels(stream_key, extent, shards, least, largest):
    def one(position, parts):
        draws = jax.random.uniform(jax.random.fold_in(jax.random.fold_in(stream_key, 6), position), (parts,), jnp.float32, least / len(shards), largest / len(shards))
        return jnp.repeat(jnp.exp(draws), extent[position] // parts).reshape((-1,) + (1,) * (len(extent) - position - 1))

    factor_of = one(*shards[0])
    for cut in shards[1:]:
        factor_of = factor_of * one(*cut)
    return factor_of


def scatter_about(key, shape, width, limit, cuts=(), held_as=jnp.bfloat16):
    gain = shard_levels(key, shape, cuts, -0.22, 0.18) if cuts else 1.0
    drawn = jax.random.normal(key, shape, jnp.float32) * width * gain
    return jnp.minimum(jnp.maximum(drawn, -limit), limit).astype(held_as)


def setup_inputs(seed: int = 0) -> dict:
    arg_keys = jax.random.split(jax.random.key(seed), 5)
    return {
        "weight": scatter_about(arg_keys[0], (M, N), 1.0, 6.0, ((0, 16), (1, 2)), jnp.float32),
        "grad": scatter_about(arg_keys[1], (M, N), 1.0, 6.0, ((0, 16), (1, 2)), jnp.float32),
        "momentum": draw_momentum(jax.random.fold_in(arg_keys[4], 71), 0),
        "right_factor": scatter_about(arg_keys[3], (N, R), N ** -0.5, 0.078125, ((0, 2),)),
    }


feedback_share = 0.05
decay_keep = 0.999
step_rate = 0.5
epsilon = 1e-06

def reference(weight, grad, momentum, right_factor):
    highest = lax.Precision.HIGHEST
    buffer = momentum + grad
    proj = jnp.dot(buffer, right_factor.astype(jnp.float32), precision=highest)
    gram = jnp.dot(proj.T, proj, precision=highest)
    factor = jnp.linalg.cholesky(gram)
    ortho = lax.linalg.triangular_solve(factor, proj, left_side=False, lower=True, transpose_a=True)
    right = jnp.dot(buffer.T, ortho, precision=highest)
    inverse = 1.0 / jnp.sqrt(lax.optimization_barrier(jnp.sum(right * right, axis=0)) + epsilon)
    new_right = (right * inverse).astype(jnp.bfloat16)
    feedback = jnp.dot(ortho, right.T, precision=highest)
    update = jnp.dot(ortho * inverse, right.T, precision=highest)
    new_momentum = buffer - feedback_share * feedback
    scale = (M * N / R) ** 0.5
    new_weight = decay_keep * weight - step_rate * scale * update
    return (new_weight, new_momentum, new_right)
```

```python
import functools

import jax
import jax.numpy as jnp
from jax import lax
from jax.experimental import pallas as pl
from jax.experimental.pallas import tpu as pltpu
from jax.sharding import PartitionSpec as P

feedback_share = 0.05
decay_keep = 0.999
step_rate = 0.5
epsilon = 1e-06
highest = lax.Precision.HIGHEST
MIB = 1 << 20


def largest_divisor(total, limit, multiple):
    for size in range(min(limit, total), 0, -1):
        if total % size == 0 and size % multiple == 0:
            return size
    return total


def split(x):
    high = x.astype(jnp.bfloat16)
    low = (x - high.astype(jnp.float32)).astype(jnp.bfloat16)
    return high, low


def mul(a, b, dims=(((1,), (0,)), ((), ()))):
    return lax.dot_general(a, b, dims, preferred_element_type=jnp.float32)


TRANSPOSED = (((0,), (0,)), ((), ()))
BOTH_LAST = (((1,), (1,)), ((), ()))


def partial_kernel(start, rows, tile, momentum, grad, right_factor, buffer, partial):
    def step(m, g, out):
        i = pl.program_id(0)
        total = m[...] + g[...]
        buffer[pl.ds(pl.multiple_of(i * tile, 8), tile), :] = total
        high, low = split(total)
        out[...] = mul(high, right_factor[...]) + mul(low, right_factor[...])

    columns = momentum.shape[1]
    pltpu.emit_pipeline(
        step,
        grid=(rows // tile,),
        in_specs=[pl.BlockSpec((tile, columns), lambda i: (i, 0))] * 2,
        out_specs=[pl.BlockSpec((tile, right_factor.shape[1]), lambda i: (i, 0))],
    )(momentum.at[pl.ds(start, rows)], grad.at[pl.ds(start, rows)], partial)


def partial_products(start, rows, momentum, grad, right_factor):
    columns, rank = right_factor.shape
    tile = largest_divisor(rows, 160, 16)
    any_space = pl.BlockSpec(memory_space=pl.ANY)
    vmem = pl.BlockSpec(memory_space=pltpu.VMEM)
    return pl.pallas_call(
        functools.partial(partial_kernel, start, rows, tile),
        out_shape=[
            pltpu.VMEM((rows, columns), jnp.float32),
            jax.ShapeDtypeStruct((rows, rank), jnp.float32),
        ],
        in_specs=[any_space, any_space, vmem],
        out_specs=[vmem, any_space],
        compiler_params=pltpu.CompilerParams(vmem_limit_bytes=16 * MIB),
        name="partial_proj",
    )(momentum, grad, right_factor)


def project_kernel(width, first, mine, theirs, buffer, *refs):
    if first:
        proj, turned, gram = refs
    else:
        turned_in, gram_in, proj, turned, gram = refs
    value = mine[...] + theirs[...]
    proj[...] = value
    square = lax.dot_general(value, value, TRANSPOSED, precision=highest, preferred_element_type=jnp.float32)
    gram[...] = square if first else gram_in[...] + square
    across = value.T
    high, low = split(across)

    @pl.loop(0, buffer.shape[1] // width)
    def _(j):
        at = pl.ds(pl.multiple_of(j * width, 128), width)
        b_high, b_low = split(buffer[:, at])
        product = mul(high, b_high) + (mul(low, b_high) + mul(high, b_low))
        turned[:, at] = product if first else turned_in[:, at] + product


def project(mine, theirs, buffer, sums):
    rows, rank = mine.shape
    columns = buffer.shape[1]
    first = sums is None
    vmem = pl.BlockSpec(memory_space=pltpu.VMEM)
    width = largest_divisor(columns, 512, 128)
    operands = (mine, theirs, buffer) + (() if first else sums)
    return pl.pallas_call(
        functools.partial(project_kernel, width, first),
        out_shape=[
            jax.ShapeDtypeStruct((rows, rank), jnp.float32),
            jax.ShapeDtypeStruct((rank, columns), jnp.float32),
            jax.ShapeDtypeStruct((rank, rank), jnp.float32),
        ],
        in_specs=[vmem] * len(operands),
        out_specs=[vmem] * 3,
        input_output_aliases={} if first else {3: 1, 4: 2},
        compiler_params=pltpu.CompilerParams(vmem_limit_bytes=24 * MIB),
        name="turned_product",
    )(*operands)


def inverse_factor_kernel(size, panel, lanes, gram, out):
    out[...] = gram[...]
    sub = lax.broadcasted_iota(jnp.int32, (panel, lanes), 0)
    lane = lax.broadcasted_iota(jnp.int32, (panel, lanes), 1)
    for j in range(0, size, panel):
        parts = [out[j : j + panel, c : c + lanes] for c in range(0, size, lanes)]
        home, at = divmod(j, lanes)
        columns = [
            jnp.broadcast_to(parts[home][:, at + q : at + q + 1], (panel, lanes)) for q in range(panel)
        ]
        inside = (lane >= at) & (lane < at + panel)
        parts[home] = jnp.where(inside, jnp.where(lane - at == sub, 1.0, 0.0), parts[home])
        for k in range(panel):
            scale = lax.rsqrt(columns[k][k : k + 1, :])
            below = jnp.where(sub > k, columns[k] * scale, 0.0)
            for q in range(k + 1, panel):
                columns[q] = columns[q] - below * (columns[q][k : k + 1, :] * scale)
            for c in range(len(parts)):
                row = parts[c][k : k + 1, :] * scale
                parts[c] = jnp.where(sub == k, row, parts[c] - below * row)
        whole = jnp.concatenate(parts, axis=1)
        out[j : j + panel, :] = whole
        after = j + panel
        if after < size:
            wide = lax.broadcasted_iota(jnp.int32, (panel, size), 1)
            factors = jnp.where(wide >= after, whole, 0.0)
            base = after // lanes * lanes
            change = lax.dot_general(
                factors[:, base:], whole, TRANSPOSED, precision=highest, preferred_element_type=jnp.float32
            )
            rest = out[after:, :]
            column = lax.broadcasted_iota(jnp.int32, rest.shape, 1)
            rest = jnp.where((column >= j) & (column < after), 0.0, rest)
            out[after:, :] = rest - change[after - base :, :]
    row = lax.broadcasted_iota(jnp.int32, (size, size), 0)
    column = lax.broadcasted_iota(jnp.int32, (size, size), 1)
    out[...] = jnp.where(column <= row, out[...], 0.0)


def inverse_factor(gram):
    size = gram.shape[0]
    vmem = pl.BlockSpec(memory_space=pltpu.VMEM)
    return pl.pallas_call(
        functools.partial(inverse_factor_kernel, size, 16, 128),
        out_shape=jax.ShapeDtypeStruct(gram.shape, jnp.float32),
        in_specs=[vmem],
        out_specs=vmem,
        compiler_params=pltpu.CompilerParams(vmem_limit_bytes=8 * MIB),
        name="inverse_factor",
    )(gram)


def outputs_kernel(tile, bounds, columns_at_once, weight, proj, back, right, inverse, *refs):
    buffers, (new_weight, new_momentum) = refs[: len(bounds)], refs[len(bounds) :]
    high, low = split(right[...])
    rank = right.shape[0]
    columns = right.shape[1]
    scale = inverse[...]
    for buffer, (start, rows) in zip(buffers, bounds):

        def step(w, p, nw, nm, buffer=buffer, rows=rows):
            i = pl.program_id(0)
            at = pl.ds(pl.multiple_of(i * tile, 8), tile)
            ortho = lax.dot_general(
                p[...], back[...], BOTH_LAST, precision=highest, preferred_element_type=jnp.float32
            )
            s_high, s_low = split(ortho * scale)
            stacked = jnp.concatenate([ortho.astype(jnp.bfloat16), s_high, s_low], axis=0)
            for c in range(0, columns, columns_at_once):
                part = slice(c, c + columns_at_once)
                both = mul(stacked, high[:, part])
                update = both[tile : 2 * tile] + (both[2 * tile :] + mul(s_high, low[:, part]))
                nm[:, part] = buffer[at, part] - feedback_share * both[:tile]
                nw[:, part] = decay_keep * w[:, part] - update

        block = pl.BlockSpec((tile, columns), lambda i: (i, 0))
        pltpu.emit_pipeline(
            step,
            grid=(rows // tile,),
            in_specs=[block, pl.BlockSpec((tile, rank), lambda i: (i, 0))],
            out_specs=[block, block],
        )(
            weight.at[pl.ds(start, rows)],
            proj.at[pl.ds(start, rows)],
            new_weight.at[pl.ds(start, rows)],
            new_momentum.at[pl.ds(start, rows)],
        )


def outputs(weight, proj, back, right, inverse, buffers, bounds):
    any_space = pl.BlockSpec(memory_space=pl.ANY)
    vmem = pl.BlockSpec(memory_space=pltpu.VMEM)
    tile = largest_divisor(bounds[0][1], 80, 16)
    columns_at_once = largest_divisor(weight.shape[1], 512, 128)
    return pl.pallas_call(
        functools.partial(outputs_kernel, tile, bounds, columns_at_once),
        out_shape=[jax.ShapeDtypeStruct(weight.shape, jnp.float32)] * 2,
        in_specs=[any_space, any_space, vmem, vmem, vmem] + [vmem] * len(buffers),
        out_specs=[any_space, any_space],
        compiler_params=pltpu.CompilerParams(vmem_limit_bytes=24 * MIB),
        name="large_outputs",
    )(weight, proj, back, right, inverse, *buffers)


def swap_pairs(x, axis, count, stride):
    return lax.ppermute(x, axis, [(i, i ^ stride) for i in range(count)])


def sum_over(x, axis, count):
    if count & (count - 1) or count < 8 or x.shape[0] % 64:
        return lax.psum(x, axis)
    index = lax.axis_index(axis)
    half = x.shape[0] // 2
    odd = index % 2
    keep = lax.dynamic_slice_in_dim(x, odd * half, half, 0)
    send = lax.dynamic_slice_in_dim(x, (1 - odd) * half, half, 0)
    keep = keep + swap_pairs(send, axis, count, 1)
    groups = [[base + first + 2 * j for j in range(4)] for base in range(0, count, 8) for first in range(2)]
    quarter = half // 4
    parts = lax.all_to_all(keep, axis, 0, 0, axis_index_groups=groups, tiled=True)
    piece = parts.reshape(4, quarter, -1).sum(axis=0)
    stride = 8
    while stride < count:
        piece = piece + swap_pairs(piece, axis, count, stride)
        stride *= 2
    copies = jnp.broadcast_to(piece[None], (4,) + piece.shape).reshape(half, -1)
    whole = lax.all_to_all(copies, axis, 0, 0, axis_index_groups=groups, tiled=True)
    other = swap_pairs(whole, axis, count, 1)
    return jnp.concatenate([jnp.where(odd == 0, whole, other), jnp.where(odd == 0, other, whole)], axis=0)


def row_bounds(rows):
    if rows % 160:
        return [(0, rows)]
    unit = rows // 5
    return [(0, unit), (unit, 2 * unit), (3 * unit, 2 * unit)]


def on_device(mesh, weight, grad, momentum, right_factor):
    row_count, col_count = mesh.shape["row"], mesh.shape["col"]
    rows, columns = weight.shape
    rank = right_factor.shape[1]
    bounds = row_bounds(rows)
    buffers, proj, sums = [], [], None
    partials = []
    for start, count in bounds:
        buffer, partial = partial_products(start, count, momentum, grad, right_factor)
        buffers.append(buffer)
        if col_count == 2:
            theirs = swap_pairs(partial, "col", 2, 1)
        else:
            theirs = lax.psum(partial, "col") - partial
        partials.append((partial, theirs))
    for buffer, (partial, theirs) in zip(buffers, partials):
        piece, *sums = project(partial, theirs, buffer, None if sums is None else tuple(sums))
        proj.append(piece)
    proj = jnp.concatenate(proj, axis=0)
    turned, gram = sums
    total = sum_over(jnp.concatenate([turned, gram], axis=1), "row", row_count)
    turned, gram = total[:, :columns], total[:, columns:]
    back = inverse_factor(gram)
    right = jnp.dot(back, turned, precision=highest)
    squares = lax.psum(jnp.sum(right * right, axis=1), "col") if col_count != 2 else None
    if squares is None:
        mine = jnp.sum(right * right, axis=1, keepdims=True).reshape(1, rank)
        squares = (mine + swap_pairs(mine, "col", 2, 1)).reshape(rank)
    inverse = 1.0 / jnp.sqrt(squares + epsilon)
    share = columns // row_count
    own = lax.dynamic_slice_in_dim(right, lax.axis_index("row") * share, share, 1)
    new_right = (own * inverse[:, None]).astype(jnp.bfloat16).T
    whole_rows, whole_columns = rows * row_count, columns * col_count
    scale = step_rate * (whole_rows * whole_columns / rank) ** 0.5
    new_weight, new_momentum = outputs(
        weight, proj, back, right, (inverse * scale).reshape(1, rank), buffers, bounds
    )
    return (new_weight, new_momentum, new_right)


def solution(mesh):
    placed = (P("row", "col"), P("row", "col"), P("row", "col"), P("col", None))
    return jax.shard_map(
        functools.partial(on_device, mesh),
        mesh=mesh,
        in_specs=placed,
        out_specs=(P("row", "col"), P("row", "col"), P(("col", "row"), None)),
        check_vma=False,
    )
```

```python
import functools
import math

import jax
import jax.numpy as jnp
from jax import lax
from jax.experimental import pallas as pl
from jax.experimental.pallas import tpu as pltpu
from jax.sharding import PartitionSpec as P

feedback_share = 0.05
decay_keep = 0.999
step_rate = 0.5
epsilon = 1e-06
highest = lax.Precision.HIGHEST
MIB = 1 << 20
VMEM = pl.BlockSpec(memory_space=pltpu.VMEM)
SMEM = pl.BlockSpec(memory_space=pltpu.SMEM)
ANY = pl.BlockSpec(memory_space=pl.ANY)


def in_hbm(x):
    return pltpu.with_memory_space_constraint(x, pltpu.HBM)


def cost(microseconds):
    return pl.CostEstimate(flops=int(microseconds * 1153e6), bytes_accessed=0, transcendentals=0)


def largest_divisor(total, limit, multiple):
    for size in range(min(limit, total), 0, -1):
        if total % size == 0 and size % multiple == 0:
            return size
    return total


def split(x):
    high = x.astype(jnp.bfloat16)
    low = (x - high.astype(jnp.float32)).astype(jnp.bfloat16)
    return high, low


def mul(a, b, dims=(((1,), (0,)), ((), ()))):
    return lax.dot_general(a, b, dims, preferred_element_type=jnp.float32)


TRANSPOSED = (((0,), (0,)), ((), ()))
BOTH_LAST = (((1,), (1,)), ((), ()))


def partial_kernel(start, counts, tile, momentum, grad, right_factor, *refs):
    count = len(counts)
    high_out, low_out, *partials = refs[-2 - count :]

    def step(m, g, h, l, out):
        high, low = split(m[...] + g[...])
        h[...] = high
        l[...] = low
        both = mul(jnp.concatenate([high, low], axis=0), right_factor[...])
        out[...] = both[:tile] + both[tile:]

    columns = momentum.shape[1]
    wide = pl.BlockSpec((tile, columns), lambda i: (i, 0))
    thin = pl.BlockSpec((tile, right_factor.shape[1]), lambda i: (i, 0))
    for rows, partial in zip(counts, partials):
        at = pl.ds(start, rows)
        pltpu.emit_pipeline(step, grid=(rows // tile,), in_specs=[wide, wide], out_specs=[wide, wide, thin])(
            momentum.at[at], grad.at[at], high_out.at[at], low_out.at[at], partial
        )
        start += rows


def partial_products(start, counts, momentum, grad, right_factor, halves, *earlier):
    columns, rank = right_factor.shape
    tile = largest_divisor(math.gcd(*counts), 192, 64)
    halves = [] if halves is None else [in_hbm(x) for x in halves]
    shapes = [pltpu.HBM(momentum.shape, jnp.bfloat16)] * 2
    shapes += [pltpu.HBM((rows, rank), jnp.float32) for rows in counts]
    out = pl.pallas_call(
        functools.partial(partial_kernel, start, counts, tile),
        out_shape=shapes,
        in_specs=[ANY, ANY, VMEM] + [ANY] * (len(halves) + len(earlier)),
        out_specs=[ANY] * len(shapes),
        input_output_aliases={3 + i: i for i in range(len(halves))},
        compiler_params=pltpu.CompilerParams(vmem_limit_bytes=16 * MIB),
        cost_estimate=cost(sum(counts) / 100),
        name="partial_proj",
    )(in_hbm(momentum), in_hbm(grad), right_factor, *halves, *earlier)
    return out[:2], out[2:]


def project_kernel(start, widths, step, first, pieces, place, high_in, low_in, before, *refs):
    count = len(widths)
    mine, theirs, refs = refs[:pieces], refs[pieces : 2 * pieces], refs[2 * pieces :]
    sums_in = None if first else refs[:count]
    proj, *sums, turned = refs[0 if first else count :]
    base = 0
    for m, t in zip(mine, theirs):
        proj[base : base + m.shape[0], :] = m[...] + t[...]
        base += m.shape[0]
    value = proj[...]
    rows, rank = value.shape
    block = rank // 8
    turned[...] = value.T
    ordered = jnp.concatenate(
        [turned[pl.ds(pl.multiple_of((place[0] ^ r) * block, block), block), :] for r in range(8)], axis=0
    )
    square = jnp.dot(ordered, value, precision=highest, preferred_element_type=jnp.float32)
    gram = slice(widths[0], widths[0] + rank)
    sums[0][:, gram] = square if first else sums_in[0][:, gram] + square
    high, low = split(ordered)
    stacked = jnp.concatenate([high, low], axis=0)

    def part(h, l):
        i = pl.program_id(0)
        both = mul(stacked, h[...])
        product = both[:rank] + (both[rank:] + mul(high, l[...]))
        before = 0
        for s, width in enumerate(widths):

            @pl.when((i >= before // step) & (i < (before + width) // step))
            def _(s=s, before=before):
                at = pl.ds(pl.multiple_of((i - before // step) * step, 128), step)
                sums[s][:, at] = product if first else sums_in[s][:, at] + product

            before += width

    at = pl.ds(start, rows)
    pltpu.emit_pipeline(
        part, grid=(sum(widths) // step,), in_specs=[pl.BlockSpec((rows, step), lambda i: (0, i))] * 2
    )(high_in.at[at], low_in.at[at])


def project(place, start, mine, theirs, halves, before, sums, widths):
    rows, rank = sum(x.shape[0] for x in mine), mine[0].shape[1]
    first = sums is None
    step = largest_divisor(math.gcd(*widths), 640, 128)
    operands = (place, *map(in_hbm, halves), before, *mine, *theirs) + (() if first else tuple(sums))
    specs = [SMEM, ANY, ANY, ANY] + [VMEM] * (len(operands) - 4)
    shapes = [jax.ShapeDtypeStruct((rows, rank), jnp.float32)]
    for s, width in enumerate(widths):
        shapes.append(jax.ShapeDtypeStruct((rank, width + (0 if s else rank)), jnp.float32))
    offset = 4 + 2 * len(mine)
    out = pl.pallas_call(
        functools.partial(project_kernel, start, widths, step, first, len(mine)),
        out_shape=shapes,
        in_specs=specs,
        out_specs=[VMEM] * len(shapes),
        input_output_aliases={} if first else {offset + i: 1 + i for i in range(len(sums))},
        scratch_shapes=[pltpu.VMEM((rank, rows), jnp.float32)],
        compiler_params=pltpu.CompilerParams(vmem_limit_bytes=20 * MIB),
        cost_estimate=cost(1 + rows / 120),
        name="turned_product",
    )(*operands)
    return out[0], list(out[1:])


def inverse_factor_kernel(size, panel, lanes, place, own, other, before, out):
    gram = slice(own.shape[1] - size, own.shape[1])
    block = size // 8
    for r in range(8):
        start = (r % 4) * block
        at = pl.ds(pl.multiple_of((place[0] ^ r) * block, block), block)
        out[at, :] = (own if r < 4 else other)[start : start + block, gram]
    sub = lax.broadcasted_iota(jnp.int32, (panel, lanes), 0)
    lane = lax.broadcasted_iota(jnp.int32, (panel, lanes), 1)
    for j in range(0, size, panel):
        parts = [out[j : j + panel, c : c + lanes] for c in range(0, size, lanes)]
        home, at = divmod(j, lanes)
        columns = [
            jnp.broadcast_to(parts[home][:, at + q : at + q + 1], (panel, lanes)) for q in range(panel)
        ]
        inside = (lane >= at) & (lane < at + panel)
        parts[home] = jnp.where(inside, jnp.where(lane - at == sub, 1.0, 0.0), parts[home])
        for k in range(panel):
            scale = lax.rsqrt(columns[k][k : k + 1, :])
            below = jnp.where(sub > k, columns[k] * scale, 0.0)
            for q in range(k + 1, panel):
                columns[q] = columns[q] - below * (columns[q][k : k + 1, :] * scale)
            for c in range(len(parts)):
                row = parts[c][k : k + 1, :] * scale
                parts[c] = jnp.where(sub == k, row, parts[c] - below * row)
        whole = jnp.concatenate(parts, axis=1)
        out[j : j + panel, :] = whole
        after = j + panel
        if after < size:
            wide = lax.broadcasted_iota(jnp.int32, (panel, size), 1)
            factors = jnp.where(wide >= after, whole, 0.0)
            base = after // lanes * lanes
            change = lax.dot_general(
                factors[:, base:], whole, TRANSPOSED, precision=highest, preferred_element_type=jnp.float32
            )
            rest = out[after:, :]
            column = lax.broadcasted_iota(jnp.int32, rest.shape, 1)
            rest = jnp.where((column >= j) & (column < after), 0.0, rest)
            out[after:, :] = rest - change[after - base :, :]
    row = lax.broadcasted_iota(jnp.int32, (size, size), 0)
    column = lax.broadcasted_iota(jnp.int32, (size, size), 1)
    out[...] = jnp.where(column <= row, out[...], 0.0)


def inverse_factor(place, own, other, before):
    size = 2 * own.shape[0]
    return pl.pallas_call(
        functools.partial(inverse_factor_kernel, size, 16, 128),
        out_shape=jax.ShapeDtypeStruct((size, size), jnp.float32),
        in_specs=[SMEM, VMEM, VMEM, ANY],
        out_specs=VMEM,
        compiler_params=pltpu.CompilerParams(vmem_limit_bytes=8 * MIB),
        cost_estimate=cost(11),
        name="inverse_factor",
    )(place, own, other, before)


def right_kernel(place, own, other, back, out, squares, ordered):
    rank, columns = out.shape
    block = rank // 8
    for r in range(8):
        source = own if r < 4 else other
        start = (r % 4) * block
        at = pl.ds(pl.multiple_of((place[0] ^ r) * block, block), block)
        ordered[at, :] = source[start : start + block, :columns]
    b_high, b_low = split(back[...])
    o_high, o_low = split(ordered[...])
    value = mul(b_high, o_high) + (mul(b_high, o_low) + mul(b_low, o_high))
    out[...] = value
    total = jnp.sum(value * value, axis=1, keepdims=True)
    squares[...] = jnp.broadcast_to(total, (rank, 128)).T[:8, :]


def right_part(place, own, other, back, columns):
    rank = back.shape[0]
    return pl.pallas_call(
        right_kernel,
        out_shape=[
            jax.ShapeDtypeStruct((rank, columns), jnp.float32),
            jax.ShapeDtypeStruct((8, rank), jnp.float32),
        ],
        in_specs=[SMEM, VMEM, VMEM, VMEM],
        out_specs=[VMEM] * 2,
        scratch_shapes=[pltpu.VMEM((rank, columns), jnp.float32)],
        compiler_params=pltpu.CompilerParams(vmem_limit_bytes=16 * MIB),
        cost_estimate=cost(2),
        name="right_columns",
    )(place, own, other, back)


def ortho_kernel(back, proj, out):
    turned_high, turned_low = split(back[...].T)
    high, low = split(proj[...])
    out[...] = mul(high, turned_high) + (mul(high, turned_low) + mul(low, turned_high))


def make_ortho(back, proj):
    rows, rank = proj.shape
    tile = largest_divisor(rows, 400, 16)
    return pl.pallas_call(
        ortho_kernel,
        out_shape=pltpu.HBM((rows, rank), jnp.float32),
        grid=(rows // tile,),
        in_specs=[pl.BlockSpec((rank, rank), lambda i: (0, 0)), pl.BlockSpec((tile, rank), lambda i: (i, 0))],
        out_specs=pl.BlockSpec((tile, rank), lambda i: (i, 0)),
        compiler_params=pltpu.CompilerParams(vmem_limit_bytes=16 * MIB),
        cost_estimate=cost(2),
        name="ortho",
    )(back, proj)


def momentum_kernel(tile, widths, ortho, high_in, low_in, *refs):
    rights, (new_momentum, highs) = refs[: len(widths)], refs[len(widths) :]
    rows, columns = new_momentum.shape
    base = 0
    for width, right in zip(widths, rights):
        highs[:, base : base + width] = right[...].astype(jnp.bfloat16)
        base += width
    step_columns = largest_divisor(columns, 512, 128)

    def step(o, h, l, out):
        high = o[...].astype(jnp.bfloat16)
        for c in range(0, columns, step_columns):
            part = slice(c, c + step_columns)
            old = h[:, part].astype(jnp.float32) + l[:, part].astype(jnp.float32)
            out[:, part] = old - feedback_share * mul(high, highs[:, part])

    wide = pl.BlockSpec((tile, columns), lambda i: (i, 0))
    thin = pl.BlockSpec((tile, ortho.shape[1]), lambda i: (i, 0))
    pltpu.emit_pipeline(step, grid=(rows // tile,), in_specs=[thin, wide, wide], out_specs=[wide])(
        ortho, high_in, low_in, new_momentum
    )


def make_momentum(ortho, halves, rights, widths):
    rows, rank = ortho.shape
    columns = sum(widths)
    tile = largest_divisor(rows, 320, 16)
    return pl.pallas_call(
        functools.partial(momentum_kernel, tile, widths),
        out_shape=pltpu.HBM((rows, columns), jnp.float32),
        in_specs=[ANY, ANY, ANY] + [VMEM] * len(widths),
        out_specs=ANY,
        scratch_shapes=[pltpu.VMEM((rank, columns), jnp.bfloat16)],
        compiler_params=pltpu.CompilerParams(vmem_limit_bytes=30 * MIB),
        cost_estimate=cost(10),
        name="new_momentum",
    )(in_hbm(ortho), *map(in_hbm, halves), *rights)


def weight_kernel(tile, widths, factor, squares, ortho, weight, *refs):
    count = len(widths)
    rights, (new_weight, highs, lows) = refs[:count], refs[count:]
    rows, columns = weight.shape
    scale = factor / jnp.sqrt(squares[0:1, :] + epsilon)
    base = 0
    for width, right in zip(widths, rights):
        highs[:, base : base + width], lows[:, base : base + width] = split(right[...])
        base += width
    step_columns = largest_divisor(columns, 512, 128)

    def step(o, old, out):
        s_high, s_low = split(o[...] * scale)
        stacked = jnp.concatenate([s_high, s_low], axis=0)
        for c in range(0, columns, step_columns):
            part = slice(c, c + step_columns)
            both = mul(stacked, highs[:, part])
            update = both[:tile] + (both[tile:] + mul(s_high, lows[:, part]))
            out[:, part] = decay_keep * old[:, part] - update

    wide = pl.BlockSpec((tile, columns), lambda i: (i, 0))
    thin = pl.BlockSpec((tile, ortho.shape[1]), lambda i: (i, 0))
    pltpu.emit_pipeline(step, grid=(rows // tile,), in_specs=[thin, wide], out_specs=[wide])(
        ortho, weight, new_weight
    )


def make_weight(factor, squares, weight, ortho, rights, widths):
    tile = largest_divisor(weight.shape[0], 320, 16)
    rank = ortho.shape[1]
    return pl.pallas_call(
        functools.partial(weight_kernel, tile, widths, factor),
        out_shape=pltpu.HBM(weight.shape, jnp.float32),
        in_specs=[VMEM, ANY, ANY] + [VMEM] * len(widths),
        out_specs=ANY,
        scratch_shapes=[pltpu.VMEM((rank, sum(widths)), jnp.bfloat16)] * 2,
        compiler_params=pltpu.CompilerParams(vmem_limit_bytes=32 * MIB),
        cost_estimate=cost(10),
        name="new_weight",
    )(squares, in_hbm(ortho), in_hbm(weight), *rights)


def swap_pairs(x, axis, count, stride):
    return lax.ppermute(x, axis, [(i, i ^ stride) for i in range(count)])


def halving_works(count):
    return count >= 8 and count & (count - 1) == 0


def add_after(x, y, before):
    def kernel(x, y, before, out):
        out[...] = x[...] + y[...]

    return pl.pallas_call(
        kernel,
        out_shape=jax.ShapeDtypeStruct(x.shape, x.dtype),
        in_specs=[VMEM, VMEM, ANY],
        out_specs=VMEM,
        compiler_params=pltpu.CompilerParams(vmem_limit_bytes=8 * MIB),
        cost_estimate=cost(0.3),
        name="add_pieces",
    )(x, y, before)


def join_after(pieces, before):
    size = pieces[0].shape[0]

    def kernel(*refs):
        for i in range(len(pieces)):
            refs[-1][i * size : (i + 1) * size, :] = refs[i][...]

    return pl.pallas_call(
        kernel,
        out_shape=jax.ShapeDtypeStruct((len(pieces) * size, pieces[0].shape[1]), pieces[0].dtype),
        in_specs=[VMEM] * len(pieces) + [ANY],
        out_specs=VMEM,
        compiler_params=pltpu.CompilerParams(vmem_limit_bytes=8 * MIB),
        cost_estimate=cost(0.5),
        name="join_pieces",
    )(*pieces, before)


def sums_over(parts, axis, count, work):
    if not halving_works(count) or len(parts) != 2:
        half = parts[0].shape[0] // 2
        totals = [lax.psum(x, axis) for x in parts]
        totals = [(x[:half], x[half:]) for x in totals]
        return totals, work(*totals[0], totals[-1][0])
    pieces = []
    for piece in parts:
        half = piece.shape[0] // 2
        piece = piece[:half] + swap_pairs(piece[half:], axis, count, 1)
        quarter = half // 4
        sent = [swap_pairs(piece[j * quarter : (j + 1) * quarter], axis, count, s) for j, s in ((2, 2), (3, 6), (1, 4))]
        pieces.append(piece[:quarter] + sent[0] + sent[1] + sent[2])
    first, second = pieces
    stride = 8
    while stride < count:
        first = add_after(first, swap_pairs(first, axis, count, stride), pieces[1])
        second = second + swap_pairs(second, axis, count, stride)
        stride *= 2

    def back(piece, before):
        others = [swap_pairs(piece, axis, count, s) for s in (2, 6, 4)]
        whole = join_after([piece, others[2], others[0], others[1]], before)
        return whole, swap_pairs(whole, axis, count, 1)

    first = back(first, second)
    result = work(*first, second)
    return [first, back(second, result)], result


def row_bounds(rows):
    if rows % (25 * 64):
        return [(0, rows)]
    unit = rows // 25
    counts = [4 * unit, 8 * unit, 9 * unit, 4 * unit]
    return [(sum(counts[:i]), count) for i, count in enumerate(counts)]


def stream_widths(columns):
    if columns % (5 * 128):
        return [columns]
    return [columns // 5 * 2, columns // 5 * 3]


def on_device(mesh, weight, grad, momentum, right_factor):
    row_count, col_count = mesh.shape["row"], mesh.shape["col"]
    rows, columns = weight.shape
    rank = right_factor.shape[1]
    bounds = row_bounds(rows)
    widths = stream_widths(columns)
    index = lax.axis_index("row")
    place = jnp.zeros((1,), jnp.int32)
    if halving_works(row_count):
        place = ((index % 2) * 4 + (index // 2 % 2) * 2 + index // 4 % 2).astype(jnp.int32).reshape(1)
    halves, partials, theirs, projs, sums = None, [], [], [], None
    for i, (start, count) in enumerate(bounds):
        if i == 3:
            proj, sums = project(place, 0, partials[:1], theirs[:1], halves, partials[-1], None, widths)
            projs.append(proj)
        earlier = (theirs[i - 2 : i - 1] if i > 1 else []) + projs
        halves, (partial,) = partial_products(start, [count], momentum, grad, right_factor, halves, *earlier)
        partials.append(partial)
        theirs.append(swap_pairs(partial, "col", 2, 1) if col_count == 2 else lax.psum(partial, "col") - partial)
    for i in range(len(projs), len(bounds)):
        proj, sums = project(
            place, bounds[i][0], [partials[i]], [theirs[i]], halves, partials[-1], sums, widths
        )
        projs.append(proj)
    turned, back = sums_over(sums, "row", row_count, functools.partial(inverse_factor, place))
    ortho = make_ortho(back, jnp.concatenate(projs, axis=0))
    rights, squares = zip(*[right_part(place, *pair, back, width) for pair, width in zip(turned, widths)])
    squares = sum(squares[1:], squares[0])
    if col_count == 2:
        squares = squares + swap_pairs(squares, "col", 2, 1)
    else:
        squares = lax.psum(squares, "col")
    new_momentum = make_momentum(ortho, halves, rights, widths)
    whole_rows, whole_columns = rows * row_count, columns * col_count
    factor = step_rate * (whole_rows * whole_columns / rank) ** 0.5
    new_weight = make_weight(factor, squares, weight, ortho, rights, widths)
    share = columns // row_count
    right = jnp.concatenate(rights, axis=1)
    inverse = 1.0 / jnp.sqrt(squares[0] + epsilon)
    own = lax.dynamic_slice_in_dim(right, index * share, share, 1)
    new_right = (own * inverse[:, None]).astype(jnp.bfloat16).T
    return (new_weight, new_momentum, new_right)


def solution(mesh):
    placed = (P("row", "col"), P("row", "col"), P("row", "col"), P("col", None))
    return jax.shard_map(
        functools.partial(on_device, mesh),
        mesh=mesh,
        in_specs=placed,
        out_specs=(P("row", "col"), P("row", "col"), P(("col", "row"), None)),
        check_vma=False,
    )
```

```python
import functools
import math

import jax
import jax.numpy as jnp
from jax import lax
from jax.experimental import pallas as pl
from jax.experimental.pallas import tpu as pltpu
from jax.sharding import PartitionSpec as P

feedback_share = 0.05
decay_keep = 0.999
step_rate = 0.5
epsilon = 1e-06
highest = lax.Precision.HIGHEST
MIB = 1 << 20
VMEM = pl.BlockSpec(memory_space=pltpu.VMEM)
SMEM = pl.BlockSpec(memory_space=pltpu.SMEM)
ANY = pl.BlockSpec(memory_space=pl.ANY)


def in_hbm(x):
    return pltpu.with_memory_space_constraint(x, pltpu.HBM)


def cost(microseconds):
    return pl.CostEstimate(flops=int(microseconds * 1153e6), bytes_accessed=0, transcendentals=0)


def largest_divisor(total, limit, multiple):
    for size in range(min(limit, total), 0, -1):
        if total % size == 0 and size % multiple == 0:
            return size
    return total


def split(x):
    high = x.astype(jnp.bfloat16)
    low = (x - high.astype(jnp.float32)).astype(jnp.bfloat16)
    return high, low


def mul(a, b, dims=(((1,), (0,)), ((), ()))):
    return lax.dot_general(a, b, dims, preferred_element_type=jnp.float32)


TRANSPOSED = (((0,), (0,)), ((), ()))
BOTH_LAST = (((1,), (1,)), ((), ()))


def partial_kernel(start, counts, tile, momentum, grad, right_factor, *refs):
    count = len(counts)
    high_out, low_out, *partials = refs[-4 - count : -2]
    factor, arrived = refs[-2:]
    copy = pltpu.make_async_copy(right_factor, factor, arrived)
    copy.start()

    def step(m, g, h, l, out):
        @pl.when(pl.program_id(0) == 0)
        def _():
            copy.wait()

        high, low = split(m[...] + g[...])
        h[...] = high
        l[...] = low
        both = mul(jnp.concatenate([high, low], axis=0), factor[...])
        out[...] = both[:tile] + both[tile:]

    columns = momentum.shape[1]
    wide = pl.BlockSpec((tile, columns), lambda i: (i, 0))
    thin = pl.BlockSpec((tile, right_factor.shape[1]), lambda i: (i, 0))
    for rows, partial in zip(counts, partials):
        at = pl.ds(start, rows)
        pltpu.emit_pipeline(step, grid=(rows // tile,), in_specs=[wide, wide], out_specs=[wide, wide, thin])(
            momentum.at[at], grad.at[at], high_out.at[at], low_out.at[at], partial
        )
        start += rows


def partial_products(start, counts, momentum, grad, right_factor, halves, *earlier):
    columns, rank = right_factor.shape
    tile = largest_divisor(math.gcd(*counts), 192, 64)
    halves = [] if halves is None else [in_hbm(x) for x in halves]
    shapes = [pltpu.HBM(momentum.shape, jnp.bfloat16)] * 2
    shapes += [pltpu.HBM((rows, rank), jnp.float32) for rows in counts]
    out = pl.pallas_call(
        functools.partial(partial_kernel, start, counts, tile),
        out_shape=shapes,
        in_specs=[ANY] * (3 + len(halves) + len(earlier)),
        out_specs=[ANY] * len(shapes),
        scratch_shapes=[pltpu.VMEM((columns, rank), right_factor.dtype), pltpu.SemaphoreType.DMA],
        input_output_aliases={3 + i: i for i in range(len(halves))},
        compiler_params=pltpu.CompilerParams(vmem_limit_bytes=16 * MIB),
        cost_estimate=cost(sum(counts) / 100),
        name="partial_proj",
    )(in_hbm(momentum), in_hbm(grad), in_hbm(right_factor), *halves, *earlier)
    return out[:2], out[2:]


def project_kernel(start, widths, step, first, pieces, place, high_in, low_in, before, *refs):
    count = len(widths)
    mine, theirs, refs = refs[:pieces], refs[pieces : 2 * pieces], refs[2 * pieces :]
    sums_in = None if first else refs[:count]
    proj, *sums, turned = refs[0 if first else count :]
    base = 0
    for m, t in zip(mine, theirs):
        proj[base : base + m.shape[0], :] = m[...] + t[...]
        base += m.shape[0]
    value = proj[...]
    rows, rank = value.shape
    block = rank // 8
    turned[...] = value.T
    ordered = jnp.concatenate(
        [turned[pl.ds(pl.multiple_of((place[0] ^ r) * block, block), block), :] for r in range(8)], axis=0
    )
    square = jnp.dot(ordered, value, precision=highest, preferred_element_type=jnp.float32)
    gram = slice(widths[0], widths[0] + rank)
    sums[0][:, gram] = square if first else sums_in[0][:, gram] + square
    high, low = split(ordered)
    stacked = jnp.concatenate([high, low], axis=0)

    def part(h, l):
        i = pl.program_id(0)
        both = mul(stacked, h[...])
        product = both[:rank] + (both[rank:] + mul(high, l[...]))
        before = 0
        for s, width in enumerate(widths):

            @pl.when((i >= before // step) & (i < (before + width) // step))
            def _(s=s, before=before):
                at = pl.ds(pl.multiple_of((i - before // step) * step, 128), step)
                sums[s][:, at] = product if first else sums_in[s][:, at] + product

            before += width

    at = pl.ds(start, rows)
    pltpu.emit_pipeline(
        part, grid=(sum(widths) // step,), in_specs=[pl.BlockSpec((rows, step), lambda i: (0, i))] * 2
    )(high_in.at[at], low_in.at[at])


def project(place, start, mine, theirs, halves, before, sums, widths):
    rows, rank = sum(x.shape[0] for x in mine), mine[0].shape[1]
    first = sums is None
    step = largest_divisor(math.gcd(*widths), 640, 128)
    operands = (place, *map(in_hbm, halves), before, *mine, *theirs) + (() if first else tuple(sums))
    specs = [SMEM, ANY, ANY, ANY] + [VMEM] * (len(operands) - 4)
    shapes = [jax.ShapeDtypeStruct((rows, rank), jnp.float32)]
    for s, width in enumerate(widths):
        shapes.append(jax.ShapeDtypeStruct((rank, width + (0 if s else rank)), jnp.float32))
    offset = 4 + 2 * len(mine)
    out = pl.pallas_call(
        functools.partial(project_kernel, start, widths, step, first, len(mine)),
        out_shape=shapes,
        in_specs=specs,
        out_specs=[VMEM] * len(shapes),
        input_output_aliases={} if first else {offset + i: 1 + i for i in range(len(sums))},
        scratch_shapes=[pltpu.VMEM((rank, rows), jnp.float32)],
        compiler_params=pltpu.CompilerParams(vmem_limit_bytes=20 * MIB),
        cost_estimate=cost(1 + rows / 120),
        name="turned_product",
    )(*operands)
    return out[0], list(out[1:])


def inverse_factor_kernel(size, panel, lanes, place, own, other, before, out):
    gram = slice(own.shape[1] - size, own.shape[1])
    block = size // 8
    for r in range(8):
        start = (r % 4) * block
        at = pl.ds(pl.multiple_of((place[0] ^ r) * block, block), block)
        out[at, :] = (own if r < 4 else other)[start : start + block, gram]
    sub = lax.broadcasted_iota(jnp.int32, (panel, lanes), 0)
    lane = lax.broadcasted_iota(jnp.int32, (panel, lanes), 1)
    for j in range(0, size, panel):
        parts = [out[j : j + panel, c : c + lanes] for c in range(0, size, lanes)]
        home, at = divmod(j, lanes)
        columns = [
            jnp.broadcast_to(parts[home][:, at + q : at + q + 1], (panel, lanes)) for q in range(panel)
        ]
        inside = (lane >= at) & (lane < at + panel)
        parts[home] = jnp.where(inside, jnp.where(lane - at == sub, 1.0, 0.0), parts[home])
        for k in range(panel):
            scale = lax.rsqrt(columns[k][k : k + 1, :])
            below = jnp.where(sub > k, columns[k] * scale, 0.0)
            for q in range(k + 1, panel):
                columns[q] = columns[q] - below * (columns[q][k : k + 1, :] * scale)
            for c in range(len(parts)):
                row = parts[c][k : k + 1, :] * scale
                parts[c] = jnp.where(sub == k, row, parts[c] - below * row)
        whole = jnp.concatenate(parts, axis=1)
        out[j : j + panel, :] = whole
        after = j + panel
        if after < size:
            wide = lax.broadcasted_iota(jnp.int32, (panel, size), 1)
            factors = jnp.where(wide >= after, whole, 0.0)
            base = after // lanes * lanes
            change = lax.dot_general(
                factors[:, base:], whole, TRANSPOSED, precision=highest, preferred_element_type=jnp.float32
            )
            rest = out[after:, :]
            column = lax.broadcasted_iota(jnp.int32, rest.shape, 1)
            rest = jnp.where((column >= j) & (column < after), 0.0, rest)
            out[after:, :] = rest - change[after - base :, :]
    row = lax.broadcasted_iota(jnp.int32, (size, size), 0)
    column = lax.broadcasted_iota(jnp.int32, (size, size), 1)
    out[...] = jnp.where(column <= row, out[...], 0.0)


def inverse_factor(place, own, other, before):
    size = 2 * own.shape[0]
    return pl.pallas_call(
        functools.partial(inverse_factor_kernel, size, 16, 128),
        out_shape=jax.ShapeDtypeStruct((size, size), jnp.float32),
        in_specs=[SMEM, VMEM, VMEM, ANY],
        out_specs=VMEM,
        compiler_params=pltpu.CompilerParams(vmem_limit_bytes=8 * MIB),
        cost_estimate=cost(11),
        name="inverse_factor",
    )(place, own, other, before)


def right_kernel(place, own, other, back, out, squares, ordered):
    rank, columns = out.shape
    block = rank // 8
    for r in range(8):
        source = own if r < 4 else other
        start = (r % 4) * block
        at = pl.ds(pl.multiple_of((place[0] ^ r) * block, block), block)
        ordered[at, :] = source[start : start + block, :columns]
    b_high, b_low = split(back[...])
    o_high, o_low = split(ordered[...])
    value = mul(b_high, o_high) + (mul(b_high, o_low) + mul(b_low, o_high))
    out[...] = value
    total = jnp.sum(value * value, axis=1, keepdims=True)
    squares[...] = jnp.broadcast_to(total, (rank, 128)).T[:8, :]


def right_part(place, own, other, back, columns):
    rank = back.shape[0]
    return pl.pallas_call(
        right_kernel,
        out_shape=[
            jax.ShapeDtypeStruct((rank, columns), jnp.float32),
            jax.ShapeDtypeStruct((8, rank), jnp.float32),
        ],
        in_specs=[SMEM, VMEM, VMEM, VMEM],
        out_specs=[VMEM] * 2,
        scratch_shapes=[pltpu.VMEM((rank, columns), jnp.float32)],
        compiler_params=pltpu.CompilerParams(vmem_limit_bytes=16 * MIB),
        cost_estimate=cost(2),
        name="right_columns",
    )(place, own, other, back)


def ortho_kernel(back, proj, out):
    turned_high, turned_low = split(back[...].T)
    high, low = split(proj[...])
    out[...] = mul(high, turned_high) + (mul(high, turned_low) + mul(low, turned_high))


def make_ortho(back, proj):
    rows, rank = proj.shape
    tile = largest_divisor(rows, 400, 16)
    return pl.pallas_call(
        ortho_kernel,
        out_shape=pltpu.HBM((rows, rank), jnp.float32),
        grid=(rows // tile,),
        in_specs=[pl.BlockSpec((rank, rank), lambda i: (0, 0)), pl.BlockSpec((tile, rank), lambda i: (i, 0))],
        out_specs=pl.BlockSpec((tile, rank), lambda i: (i, 0)),
        compiler_params=pltpu.CompilerParams(vmem_limit_bytes=16 * MIB),
        cost_estimate=cost(2),
        name="ortho",
    )(back, proj)


def momentum_kernel(tile, widths, ortho, high_in, low_in, *refs):
    rights, (before, new_momentum, highs) = refs[: len(widths)], refs[len(widths) :]
    rows, columns = new_momentum.shape
    base = 0
    for width, right in zip(widths, rights):
        highs[:, base : base + width] = right[...].astype(jnp.bfloat16)
        base += width
    step_columns = largest_divisor(columns, 512, 128)

    def step(o, h, l, out):
        high = o[...].astype(jnp.bfloat16)
        for c in range(0, columns, step_columns):
            part = slice(c, c + step_columns)
            old = h[:, part].astype(jnp.float32) + l[:, part].astype(jnp.float32)
            out[:, part] = old - feedback_share * mul(high, highs[:, part])

    wide = pl.BlockSpec((tile, columns), lambda i: (i, 0))
    thin = pl.BlockSpec((tile, ortho.shape[1]), lambda i: (i, 0))
    pltpu.emit_pipeline(step, grid=(rows // tile,), in_specs=[thin, wide, wide], out_specs=[wide])(
        ortho, high_in, low_in, new_momentum
    )


def make_momentum(ortho, halves, rights, widths, before):
    rows, rank = ortho.shape
    columns = sum(widths)
    tile = largest_divisor(rows, 320, 16)
    return pl.pallas_call(
        functools.partial(momentum_kernel, tile, widths),
        out_shape=pltpu.HBM((rows, columns), jnp.float32),
        in_specs=[ANY, ANY, ANY] + [VMEM] * len(widths) + [ANY],
        out_specs=ANY,
        scratch_shapes=[pltpu.VMEM((rank, columns), jnp.bfloat16)],
        compiler_params=pltpu.CompilerParams(vmem_limit_bytes=30 * MIB),
        cost_estimate=cost(10),
        name="new_momentum",
    )(in_hbm(ortho), *halves, *rights, in_hbm(before))


def weight_kernel(tile, widths, factor, squares, ortho, weight, *refs):
    count = len(widths)
    rights, (new_weight, highs, lows) = refs[:count], refs[count:]
    rows, columns = weight.shape
    scale = factor / jnp.sqrt(squares[0:1, :] + epsilon)
    base = 0
    for width, right in zip(widths, rights):
        highs[:, base : base + width], lows[:, base : base + width] = split(right[...])
        base += width
    step_columns = largest_divisor(columns, 512, 128)

    def step(o, old, out):
        s_high, s_low = split(o[...] * scale)
        stacked = jnp.concatenate([s_high, s_low], axis=0)
        for c in range(0, columns, step_columns):
            part = slice(c, c + step_columns)
            both = mul(stacked, highs[:, part])
            update = both[:tile] + (both[tile:] + mul(s_high, lows[:, part]))
            out[:, part] = decay_keep * old[:, part] - update

    wide = pl.BlockSpec((tile, columns), lambda i: (i, 0))
    thin = pl.BlockSpec((tile, ortho.shape[1]), lambda i: (i, 0))
    pltpu.emit_pipeline(step, grid=(rows // tile,), in_specs=[thin, wide], out_specs=[wide])(
        ortho, weight, new_weight
    )


def make_weight(factor, squares, weight, ortho, rights, widths):
    tile = largest_divisor(weight.shape[0], 320, 16)
    rank = ortho.shape[1]
    return pl.pallas_call(
        functools.partial(weight_kernel, tile, widths, factor),
        out_shape=pltpu.HBM(weight.shape, jnp.float32),
        in_specs=[VMEM, ANY, ANY] + [VMEM] * len(widths),
        out_specs=ANY,
        scratch_shapes=[pltpu.VMEM((rank, sum(widths)), jnp.bfloat16)] * 2,
        compiler_params=pltpu.CompilerParams(vmem_limit_bytes=32 * MIB),
        cost_estimate=cost(10),
        name="new_weight",
    )(squares, in_hbm(ortho), in_hbm(weight), *rights)


def swap_pairs(x, axis, count, stride):
    return lax.ppermute(x, axis, [(i, i ^ stride) for i in range(count)])


def halving_works(count):
    return count >= 8 and count & (count - 1) == 0


def add_after(x, y, before):
    def kernel(x, y, before, out):
        out[...] = x[...] + y[...]

    return pl.pallas_call(
        kernel,
        out_shape=jax.ShapeDtypeStruct(x.shape, x.dtype),
        in_specs=[VMEM, VMEM, ANY],
        out_specs=VMEM,
        compiler_params=pltpu.CompilerParams(vmem_limit_bytes=8 * MIB),
        cost_estimate=cost(0.3),
        name="add_pieces",
    )(x, y, before)


def join_after(pieces, before):
    size = pieces[0].shape[0]

    def kernel(*refs):
        for i in range(len(pieces)):
            refs[-1][i * size : (i + 1) * size, :] = refs[i][...]

    return pl.pallas_call(
        kernel,
        out_shape=jax.ShapeDtypeStruct((len(pieces) * size, pieces[0].shape[1]), pieces[0].dtype),
        in_specs=[VMEM] * len(pieces) + [ANY],
        out_specs=VMEM,
        compiler_params=pltpu.CompilerParams(vmem_limit_bytes=8 * MIB),
        cost_estimate=cost(0.5),
        name="join_pieces",
    )(*pieces, before)


def sums_over(parts, axis, count, work):
    if not halving_works(count) or len(parts) != 2:
        half = parts[0].shape[0] // 2
        totals = [lax.psum(x, axis) for x in parts]
        totals = [(x[:half], x[half:]) for x in totals]
        return totals, work(*totals[0], totals[-1][0])
    pieces = []
    for piece in parts:
        half = piece.shape[0] // 2
        piece = piece[:half] + swap_pairs(piece[half:], axis, count, 1)
        quarter = half // 4
        sent = [swap_pairs(piece[j * quarter : (j + 1) * quarter], axis, count, s) for j, s in ((2, 2), (3, 6), (1, 4))]
        pieces.append(piece[:quarter] + sent[0] + sent[1] + sent[2])
    first, second = pieces
    stride = 8
    while stride < count:
        first = add_after(first, swap_pairs(first, axis, count, stride), pieces[1])
        second = second + swap_pairs(second, axis, count, stride)
        stride *= 2

    def back(piece, before):
        others = [swap_pairs(piece, axis, count, s) for s in (2, 6, 4)]
        whole = join_after([piece, others[2], others[0], others[1]], before)
        return whole, swap_pairs(whole, axis, count, 1)

    first = back(first, second)
    result = work(*first, second)
    return [first, back(second, result)], result


def row_bounds(rows):
    if rows % (25 * 64):
        return [(0, rows)]
    unit = rows // 25
    counts = [4 * unit, 8 * unit, 9 * unit, 4 * unit]
    return [(sum(counts[:i]), count) for i, count in enumerate(counts)]


def stream_widths(columns):
    if columns % (5 * 128):
        return [columns]
    return [columns // 5 * 2, columns // 5 * 3]


def on_device(mesh, weight, grad, momentum, right_factor):
    row_count, col_count = mesh.shape["row"], mesh.shape["col"]
    rows, columns = weight.shape
    rank = right_factor.shape[1]
    bounds = row_bounds(rows)
    widths = stream_widths(columns)
    index = lax.axis_index("row")
    place = jnp.zeros((1,), jnp.int32)
    if halving_works(row_count):
        place = ((index % 2) * 4 + (index // 2 % 2) * 2 + index // 4 % 2).astype(jnp.int32).reshape(1)
    halves, partials, theirs, projs, sums = None, [], [], [], None
    for i, (start, count) in enumerate(bounds):
        earlier = theirs[i - 2 : i - 1] if i > 1 else []
        halves, (partial,) = partial_products(start, [count], momentum, grad, right_factor, halves, *earlier)
        partials.append(partial)
        theirs.append(swap_pairs(partial, "col", 2, 1) if col_count == 2 else lax.psum(partial, "col") - partial)
    for group in ([0, 1], [2], [3]) if len(bounds) == 4 else [[i] for i in range(len(bounds))]:
        mine, other = [partials[i] for i in group], [theirs[i] for i in group]
        proj, sums = project(place, bounds[group[0]][0], mine, other, halves, partials[-1], sums, widths)
        projs.append(proj)
    turned, back = sums_over(sums, "row", row_count, functools.partial(inverse_factor, place))
    ortho = make_ortho(back, jnp.concatenate(projs, axis=0))
    rights, squares = zip(*[right_part(place, *pair, back, width) for pair, width in zip(turned, widths)])
    squares = sum(squares[1:], squares[0])
    if col_count == 2:
        squares = squares + swap_pairs(squares, "col", 2, 1)
    else:
        squares = lax.psum(squares, "col")
    whole_rows, whole_columns = rows * row_count, columns * col_count
    factor = step_rate * (whole_rows * whole_columns / rank) ** 0.5
    new_weight = make_weight(factor, squares, weight, ortho, rights, widths)
    new_momentum = make_momentum(ortho, halves, rights, widths, new_weight)
    share = columns // row_count
    right = jnp.concatenate(rights, axis=1)
    inverse = 1.0 / jnp.sqrt(squares[0] + epsilon)
    own = lax.dynamic_slice_in_dim(right, index * share, share, 1)
    new_right = (own * inverse[:, None]).astype(jnp.bfloat16).T
    return (new_weight, new_momentum, new_right)


def solution(mesh):
    placed = (P("row", "col"), P("row", "col"), P("row", "col"), P("col", None))
    return jax.shard_map(
        functools.partial(on_device, mesh),
        mesh=mesh,
        in_specs=placed,
        out_specs=(P("row", "col"), P("row", "col"), P(("col", "row"), None)),
        check_vma=False,
    )
```

```python
import functools
import math

import jax
import jax.numpy as jnp
from jax import lax
from jax.experimental import pallas as pl
from jax.experimental.pallas import tpu as pltpu
from jax.sharding import PartitionSpec as P

feedback_share = 0.05
decay_keep = 0.999
step_rate = 0.5
epsilon = 1e-06
highest = lax.Precision.HIGHEST
MIB = 1 << 20
VMEM = pl.BlockSpec(memory_space=pltpu.VMEM)
SMEM = pl.BlockSpec(memory_space=pltpu.SMEM)
ANY = pl.BlockSpec(memory_space=pl.ANY)


def in_hbm(x):
    return pltpu.with_memory_space_constraint(x, pltpu.HBM)


def cost(microseconds):
    return pl.CostEstimate(flops=int(microseconds * 1153e6), bytes_accessed=0, transcendentals=0)


def largest_divisor(total, limit, multiple):
    for size in range(min(limit, total), 0, -1):
        if total % size == 0 and size % multiple == 0:
            return size
    return total


def split(x):
    high = x.astype(jnp.bfloat16)
    low = (x - high.astype(jnp.float32)).astype(jnp.bfloat16)
    return high, low


def mul(a, b, dims=(((1,), (0,)), ((), ()))):
    return lax.dot_general(a, b, dims, preferred_element_type=jnp.float32)


TRANSPOSED = (((0,), (0,)), ((), ()))
BOTH_LAST = (((1,), (1,)), ((), ()))


def partial_kernel(start, counts, tile, momentum, grad, right_factor, *refs):
    count = len(counts)
    high_out, low_out, *partials = refs[-4 - count : -2]
    factor, arrived = refs[-2:]
    copy = pltpu.make_async_copy(right_factor, factor, arrived)
    copy.start()

    def step(m, g, h, l, out):
        @pl.when(pl.program_id(0) == 0)
        def _():
            copy.wait()

        high, low = split(m[...] + g[...])
        h[...] = high
        l[...] = low
        both = mul(jnp.concatenate([high, low], axis=0), factor[...])
        out[...] = both[:tile] + both[tile:]

    columns = momentum.shape[1]
    wide = pl.BlockSpec((tile, columns), lambda i: (i, 0))
    thin = pl.BlockSpec((tile, right_factor.shape[1]), lambda i: (i, 0))
    for rows, partial in zip(counts, partials):
        at = pl.ds(start, rows)
        pltpu.emit_pipeline(step, grid=(rows // tile,), in_specs=[wide, wide], out_specs=[wide, wide, thin])(
            momentum.at[at], grad.at[at], high_out.at[at], low_out.at[at], partial
        )
        start += rows


def partial_products(start, counts, momentum, grad, right_factor, halves, *earlier):
    columns, rank = right_factor.shape
    tile = largest_divisor(math.gcd(*counts), 192, 64)
    halves = [] if halves is None else [in_hbm(x) for x in halves]
    shapes = [pltpu.HBM(momentum.shape, jnp.bfloat16)] * 2
    shapes += [pltpu.HBM((rows, rank), jnp.float32) for rows in counts]
    out = pl.pallas_call(
        functools.partial(partial_kernel, start, counts, tile),
        out_shape=shapes,
        in_specs=[ANY] * (3 + len(halves) + len(earlier)),
        out_specs=[ANY] * len(shapes),
        scratch_shapes=[pltpu.VMEM((columns, rank), right_factor.dtype), pltpu.SemaphoreType.DMA],
        input_output_aliases={3 + i: i for i in range(len(halves))},
        compiler_params=pltpu.CompilerParams(vmem_limit_bytes=16 * MIB),
        cost_estimate=cost(sum(counts) / 100),
        name="partial_proj",
    )(in_hbm(momentum), in_hbm(grad), in_hbm(right_factor), *halves, *earlier)
    return out[:2], out[2:]


def project_kernel(start, widths, step, first, pieces, place, high_in, low_in, before, *refs):
    count = len(widths)
    mine, theirs, refs = refs[:pieces], refs[pieces : 2 * pieces], refs[2 * pieces :]
    sums_in = None if first else refs[:count]
    proj, *sums, turned = refs[0 if first else count :]
    base = 0
    for m, t in zip(mine, theirs):
        proj[base : base + m.shape[0], :] = m[...] + t[...]
        base += m.shape[0]
    value = proj[...]
    rows, rank = value.shape
    block = rank // 8
    turned[...] = value.T
    ordered = jnp.concatenate(
        [turned[pl.ds(pl.multiple_of((place[0] ^ r) * block, block), block), :] for r in range(8)], axis=0
    )
    square = jnp.dot(ordered, value, precision=highest, preferred_element_type=jnp.float32)
    gram = slice(widths[0], widths[0] + rank)
    sums[0][:, gram] = square if first else sums_in[0][:, gram] + square
    high, low = split(ordered)
    stacked = jnp.concatenate([high, low], axis=0)

    def part(h, l):
        i = pl.program_id(0)
        both = mul(stacked, h[...])
        product = both[:rank] + (both[rank:] + mul(high, l[...]))
        before = 0
        for s, width in enumerate(widths):

            @pl.when((i >= before // step) & (i < (before + width) // step))
            def _(s=s, before=before):
                at = pl.ds(pl.multiple_of((i - before // step) * step, 128), step)
                sums[s][:, at] = product if first else sums_in[s][:, at] + product

            before += width

    at = pl.ds(start, rows)
    pltpu.emit_pipeline(
        part, grid=(sum(widths) // step,), in_specs=[pl.BlockSpec((rows, step), lambda i: (0, i))] * 2
    )(high_in.at[at], low_in.at[at])


def project(place, start, mine, theirs, halves, before, sums, widths):
    rows, rank = sum(x.shape[0] for x in mine), mine[0].shape[1]
    first = sums is None
    step = largest_divisor(math.gcd(*widths), 640, 128)
    operands = (place, *map(in_hbm, halves), before, *mine, *theirs) + (() if first else tuple(sums))
    specs = [SMEM, ANY, ANY, ANY] + [VMEM] * (len(operands) - 4)
    shapes = [jax.ShapeDtypeStruct((rows, rank), jnp.float32)]
    for s, width in enumerate(widths):
        shapes.append(jax.ShapeDtypeStruct((rank, width + (0 if s else rank)), jnp.float32))
    offset = 4 + 2 * len(mine)
    out = pl.pallas_call(
        functools.partial(project_kernel, start, widths, step, first, len(mine)),
        out_shape=shapes,
        in_specs=specs,
        out_specs=[VMEM] * len(shapes),
        input_output_aliases={} if first else {offset + i: 1 + i for i in range(len(sums))},
        scratch_shapes=[pltpu.VMEM((rank, rows), jnp.float32)],
        compiler_params=pltpu.CompilerParams(vmem_limit_bytes=20 * MIB),
        cost_estimate=cost(1 + rows / 120),
        name="turned_product",
    )(*operands)
    return out[0], list(out[1:])


def inverse_factor_kernel(size, panel, lanes, place, own, other, before, out):
    gram = slice(own.shape[1] - size, own.shape[1])
    block = size // 8
    for r in range(8):
        start = (r % 4) * block
        at = pl.ds(pl.multiple_of((place[0] ^ r) * block, block), block)
        out[at, :] = (own if r < 4 else other)[start : start + block, gram]
    sub = lax.broadcasted_iota(jnp.int32, (panel, lanes), 0)
    lane = lax.broadcasted_iota(jnp.int32, (panel, lanes), 1)
    for j in range(0, size, panel):
        parts = [out[j : j + panel, c : c + lanes] for c in range(0, size, lanes)]
        home, at = divmod(j, lanes)
        columns = [
            jnp.broadcast_to(parts[home][:, at + q : at + q + 1], (panel, lanes)) for q in range(panel)
        ]
        inside = (lane >= at) & (lane < at + panel)
        parts[home] = jnp.where(inside, jnp.where(lane - at == sub, 1.0, 0.0), parts[home])
        for k in range(panel):
            scale = lax.rsqrt(columns[k][k : k + 1, :])
            below = jnp.where(sub > k, columns[k] * scale, 0.0)
            for q in range(k + 1, panel):
                columns[q] = columns[q] - below * (columns[q][k : k + 1, :] * scale)
            for c in range(len(parts)):
                row = parts[c][k : k + 1, :] * scale
                parts[c] = jnp.where(sub == k, row, parts[c] - below * row)
        whole = jnp.concatenate(parts, axis=1)
        out[j : j + panel, :] = whole
        after = j + panel
        if after < size:
            wide = lax.broadcasted_iota(jnp.int32, (panel, size), 1)
            factors = jnp.where(wide >= after, whole, 0.0)
            base = after // lanes * lanes
            change = lax.dot_general(
                factors[:, base:], whole, TRANSPOSED, precision=highest, preferred_element_type=jnp.float32
            )
            rest = out[after:, :]
            column = lax.broadcasted_iota(jnp.int32, rest.shape, 1)
            rest = jnp.where((column >= j) & (column < after), 0.0, rest)
            out[after:, :] = rest - change[after - base :, :]
    row = lax.broadcasted_iota(jnp.int32, (size, size), 0)
    column = lax.broadcasted_iota(jnp.int32, (size, size), 1)
    out[...] = jnp.where(column <= row, out[...], 0.0)


def inverse_factor(place, own, other, before):
    size = 2 * own.shape[0]
    return pl.pallas_call(
        functools.partial(inverse_factor_kernel, size, 32, 128),
        out_shape=jax.ShapeDtypeStruct((size, size), jnp.float32),
        in_specs=[SMEM, VMEM, VMEM, ANY],
        out_specs=VMEM,
        compiler_params=pltpu.CompilerParams(vmem_limit_bytes=8 * MIB),
        cost_estimate=cost(11),
        name="inverse_factor",
    )(place, own, other, before)


def right_kernel(place, own, other, back, out, squares, ordered):
    rank, columns = out.shape
    block = rank // 8
    for r in range(8):
        source = own if r < 4 else other
        start = (r % 4) * block
        at = pl.ds(pl.multiple_of((place[0] ^ r) * block, block), block)
        ordered[at, :] = source[start : start + block, :columns]
    b_high, b_low = split(back[...])
    o_high, o_low = split(ordered[...])
    value = mul(b_high, o_high) + (mul(b_high, o_low) + mul(b_low, o_high))
    out[...] = value
    total = jnp.sum(value * value, axis=1, keepdims=True)
    squares[...] = jnp.broadcast_to(total, (rank, 128)).T[:8, :]


def right_part(place, own, other, back, columns):
    rank = back.shape[0]
    return pl.pallas_call(
        right_kernel,
        out_shape=[
            jax.ShapeDtypeStruct((rank, columns), jnp.float32),
            jax.ShapeDtypeStruct((8, rank), jnp.float32),
        ],
        in_specs=[SMEM, VMEM, VMEM, VMEM],
        out_specs=[VMEM] * 2,
        scratch_shapes=[pltpu.VMEM((rank, columns), jnp.float32)],
        compiler_params=pltpu.CompilerParams(vmem_limit_bytes=16 * MIB),
        cost_estimate=cost(2),
        name="right_columns",
    )(place, own, other, back)


def ortho_kernel(back, proj, out):
    turned_high, turned_low = split(back[...].T)
    high, low = split(proj[...])
    out[...] = mul(high, turned_high) + (mul(high, turned_low) + mul(low, turned_high))


def make_ortho(back, proj):
    rows, rank = proj.shape
    tile = largest_divisor(rows, 400, 16)
    return pl.pallas_call(
        ortho_kernel,
        out_shape=pltpu.HBM((rows, rank), jnp.float32),
        grid=(rows // tile,),
        in_specs=[pl.BlockSpec((rank, rank), lambda i: (0, 0)), pl.BlockSpec((tile, rank), lambda i: (i, 0))],
        out_specs=pl.BlockSpec((tile, rank), lambda i: (i, 0)),
        compiler_params=pltpu.CompilerParams(vmem_limit_bytes=16 * MIB),
        cost_estimate=cost(2),
        name="ortho",
    )(back, proj)


def momentum_kernel(tile, widths, ortho, high_in, low_in, *refs):
    rights, (before, new_momentum, highs) = refs[: len(widths)], refs[len(widths) :]
    rows, columns = new_momentum.shape
    base = 0
    for width, right in zip(widths, rights):
        highs[:, base : base + width] = right[...].astype(jnp.bfloat16)
        base += width
    step_columns = largest_divisor(columns, 512, 128)

    def step(o, h, l, out):
        high = o[...].astype(jnp.bfloat16)
        for c in range(0, columns, step_columns):
            part = slice(c, c + step_columns)
            old = h[:, part].astype(jnp.float32) + l[:, part].astype(jnp.float32)
            out[:, part] = old - feedback_share * mul(high, highs[:, part])

    wide = pl.BlockSpec((tile, columns), lambda i: (i, 0))
    thin = pl.BlockSpec((tile, ortho.shape[1]), lambda i: (i, 0))
    pltpu.emit_pipeline(step, grid=(rows // tile,), in_specs=[thin, wide, wide], out_specs=[wide])(
        ortho, high_in, low_in, new_momentum
    )


def make_momentum(ortho, halves, rights, widths, before):
    rows, rank = ortho.shape
    columns = sum(widths)
    tile = largest_divisor(rows, 320, 16)
    return pl.pallas_call(
        functools.partial(momentum_kernel, tile, widths),
        out_shape=pltpu.HBM((rows, columns), jnp.float32),
        in_specs=[ANY, ANY, ANY] + [VMEM] * len(widths) + [ANY],
        out_specs=ANY,
        scratch_shapes=[pltpu.VMEM((rank, columns), jnp.bfloat16)],
        compiler_params=pltpu.CompilerParams(vmem_limit_bytes=30 * MIB),
        cost_estimate=cost(10),
        name="new_momentum",
    )(in_hbm(ortho), *halves, *rights, in_hbm(before))


def weight_kernel(tile, widths, factor, squares, ortho, weight, *refs):
    count = len(widths)
    rights, (new_weight, highs, lows) = refs[:count], refs[count:]
    rows, columns = weight.shape
    scale = factor / jnp.sqrt(squares[0:1, :] + epsilon)
    base = 0
    for width, right in zip(widths, rights):
        highs[:, base : base + width], lows[:, base : base + width] = split(right[...])
        base += width
    step_columns = largest_divisor(columns, 512, 128)

    def step(o, old, out):
        s_high, s_low = split(o[...] * scale)
        stacked = jnp.concatenate([s_high, s_low], axis=0)
        for c in range(0, columns, step_columns):
            part = slice(c, c + step_columns)
            both = mul(stacked, highs[:, part])
            update = both[:tile] + (both[tile:] + mul(s_high, lows[:, part]))
            out[:, part] = decay_keep * old[:, part] - update

    wide = pl.BlockSpec((tile, columns), lambda i: (i, 0))
    thin = pl.BlockSpec((tile, ortho.shape[1]), lambda i: (i, 0))
    pltpu.emit_pipeline(step, grid=(rows // tile,), in_specs=[thin, wide], out_specs=[wide])(
        ortho, weight, new_weight
    )


def make_weight(factor, squares, weight, ortho, rights, widths):
    tile = largest_divisor(weight.shape[0], 320, 16)
    rank = ortho.shape[1]
    return pl.pallas_call(
        functools.partial(weight_kernel, tile, widths, factor),
        out_shape=pltpu.HBM(weight.shape, jnp.float32),
        in_specs=[VMEM, ANY, ANY] + [VMEM] * len(widths),
        out_specs=ANY,
        scratch_shapes=[pltpu.VMEM((rank, sum(widths)), jnp.bfloat16)] * 2,
        compiler_params=pltpu.CompilerParams(vmem_limit_bytes=32 * MIB),
        cost_estimate=cost(10),
        name="new_weight",
    )(squares, in_hbm(ortho), in_hbm(weight), *rights)


def swap_pairs(x, axis, count, stride):
    return lax.ppermute(x, axis, [(i, i ^ stride) for i in range(count)])


def halving_works(count):
    return count >= 8 and count & (count - 1) == 0


def add_after(x, y, before):
    def kernel(x, y, before, out):
        out[...] = x[...] + y[...]

    return pl.pallas_call(
        kernel,
        out_shape=jax.ShapeDtypeStruct(x.shape, x.dtype),
        in_specs=[VMEM, VMEM, ANY],
        out_specs=VMEM,
        compiler_params=pltpu.CompilerParams(vmem_limit_bytes=8 * MIB),
        cost_estimate=cost(0.3),
        name="add_pieces",
    )(x, y, before)


def join_after(pieces, before):
    size = pieces[0].shape[0]

    def kernel(*refs):
        for i in range(len(pieces)):
            refs[-1][i * size : (i + 1) * size, :] = refs[i][...]

    return pl.pallas_call(
        kernel,
        out_shape=jax.ShapeDtypeStruct((len(pieces) * size, pieces[0].shape[1]), pieces[0].dtype),
        in_specs=[VMEM] * len(pieces) + [ANY],
        out_specs=VMEM,
        compiler_params=pltpu.CompilerParams(vmem_limit_bytes=8 * MIB),
        cost_estimate=cost(0.5),
        name="join_pieces",
    )(*pieces, before)


def sums_over(parts, axis, count, work):
    if not halving_works(count) or len(parts) != 2:
        half = parts[0].shape[0] // 2
        totals = [lax.psum(x, axis) for x in parts]
        totals = [(x[:half], x[half:]) for x in totals]
        return totals, work(*totals[0], totals[-1][0])
    pieces = []
    for piece in parts:
        half = piece.shape[0] // 2
        piece = piece[:half] + swap_pairs(piece[half:], axis, count, 1)
        quarter = half // 4
        sent = [swap_pairs(piece[j * quarter : (j + 1) * quarter], axis, count, s) for j, s in ((2, 2), (3, 6), (1, 4))]
        pieces.append(piece[:quarter] + sent[0] + sent[1] + sent[2])
    first, second = pieces
    stride = 8
    while stride < count:
        first = add_after(first, swap_pairs(first, axis, count, stride), pieces[1])
        second = second + swap_pairs(second, axis, count, stride)
        stride *= 2

    def back(piece, before):
        others = [swap_pairs(piece, axis, count, s) for s in (2, 6, 4)]
        whole = join_after([piece, others[2], others[0], others[1]], before)
        return whole, swap_pairs(whole, axis, count, 1)

    first = back(first, second)
    result = work(*first, second)
    return [first, back(second, result)], result


def row_bounds(rows):
    if rows % (25 * 64):
        return [(0, rows)]
    unit = rows // 25
    counts = [4 * unit, 8 * unit, 9 * unit, 4 * unit]
    return [(sum(counts[:i]), count) for i, count in enumerate(counts)]


def stream_widths(columns):
    if columns % (5 * 128):
        return [columns]
    return [columns // 5 * 2, columns // 5 * 3]


def on_device(mesh, weight, grad, momentum, right_factor):
    row_count, col_count = mesh.shape["row"], mesh.shape["col"]
    rows, columns = weight.shape
    rank = right_factor.shape[1]
    bounds = row_bounds(rows)
    widths = stream_widths(columns)
    index = lax.axis_index("row")
    place = jnp.zeros((1,), jnp.int32)
    if halving_works(row_count):
        place = ((index % 2) * 4 + (index // 2 % 2) * 2 + index // 4 % 2).astype(jnp.int32).reshape(1)
    halves, partials, theirs, projs, sums = None, [], [], [], None
    for i, (start, count) in enumerate(bounds):
        earlier = theirs[i - 2 : i - 1] if i > 1 else []
        halves, (partial,) = partial_products(start, [count], momentum, grad, right_factor, halves, *earlier)
        partials.append(partial)
        theirs.append(swap_pairs(partial, "col", 2, 1) if col_count == 2 else lax.psum(partial, "col") - partial)
    for group in ([0, 1], [2], [3]) if len(bounds) == 4 else [[i] for i in range(len(bounds))]:
        mine, other = [partials[i] for i in group], [theirs[i] for i in group]
        proj, sums = project(place, bounds[group[0]][0], mine, other, halves, partials[-1], sums, widths)
        projs.append(proj)
    turned, back = sums_over(sums, "row", row_count, functools.partial(inverse_factor, place))
    ortho = make_ortho(back, jnp.concatenate(projs, axis=0))
    rights, squares = zip(*[right_part(place, *pair, back, width) for pair, width in zip(turned, widths)])
    squares = sum(squares[1:], squares[0])
    if col_count == 2:
        squares = squares + swap_pairs(squares, "col", 2, 1)
    else:
        squares = lax.psum(squares, "col")
    whole_rows, whole_columns = rows * row_count, columns * col_count
    factor = step_rate * (whole_rows * whole_columns / rank) ** 0.5
    new_weight = make_weight(factor, squares, weight, ortho, rights, widths)
    new_momentum = make_momentum(ortho, halves, rights, widths, new_weight)
    share = columns // row_count
    right = jnp.concatenate(rights, axis=1)
    inverse = 1.0 / jnp.sqrt(squares[0] + epsilon)
    own = lax.dynamic_slice_in_dim(right, index * share, share, 1)
    new_right = (own * inverse[:, None]).astype(jnp.bfloat16).T
    return (new_weight, new_momentum, new_right)


def solution(mesh):
    placed = (P("row", "col"), P("row", "col"), P("row", "col"), P("col", None))
    return jax.shard_map(
        functools.partial(on_device, mesh),
        mesh=mesh,
        in_specs=placed,
        out_specs=(P("row", "col"), P("row", "col"), P(("col", "row"), None)),
        check_vma=False,
    )
```
